128 devices in a mesh: ctx: 16 (over x_lo, y, core), ch: 8 (over x_hi, z).
Axes of the slice: x: 4 (x_hi: 2, x_lo: 2; x = x_hi * 2 + x_lo), y: 4, z: 4, core: 2. Of those that a mesh axis runs over, the one named last changes fastest.
Arguments:
- query_branch: bfloat16 [4096, 8192], P('ctx', 'ch'), may hold values from -6 to 6
- key_raw: bfloat16 [4096, 8192], P('ctx', 'ch'), may hold values from -6 to 6
- value_branch: bfloat16 [4096, 8192], P('ctx', 'ch'), may hold values from -6 to 6
- conv_out: bfloat16 [4096, 8192], P('ctx', 'ch'), may hold values from -6 to 6
- out_grad: bfloat16 [4096, 8192], P('ctx', 'ch'), may hold values from -18 to 18
- long_filter: bfloat16 [4096, 8192], P('ctx', 'ch'), may hold values from -0.09375 to 0.09375
- short_filter: float32 [3, 8192], P(None, 'ch'), may hold values from -3 to 3
Outputs:
- query_grad: bfloat16 [4096, 8192], P('ctx', 'ch')
- key_raw_grad: bfloat16 [4096, 8192], P('ctx', 'ch')
- value_grad: bfloat16 [4096, 8192], P('ctx', 'ch')
- filter_grad: float32 [4096, 8192], P('ctx', 'ch')
- short_grad: float32 [3, 8192], P(None, 'ch')
The draws below stay inside these ranges and needn't reach their ends.
All inputs are finite; a program needn't handle non-finite values.
Results may differ from the reference program's by a relative error of at most 0.0049.
Values may be sent and summed in bfloat16 or wider, within the bound.
A program may use at most 128 MiB of HBM per device.

```python
import math
import jax
import jax.numpy as jnp
from jax import lax

D = 8192
TAPS = 3
SEQ = 4096


def draw_out_grad(key, part):
    key = jax.random.fold_in(key, 7)
    base_key, chan_key = jax.random.split(key, 2)
    chan_scale = 0.3 * jnp.exp(jax.random.uniform(chan_key, (D,), jnp.float32, 0.0, math.log(10.0)))
    base = jnp.clip(jax.random.normal(base_key, (SEQ, D), jnp.float32), -6.0, 6.0)
    values = base * chan_scale[None, :]
    return values.astype(jnp.bfloat16)


def block_levels(key, dims, pieces, smallest, largest):
    factor_of, own = 1.0, jax.random.fold_in(key, 6)
    for axis_at, parts in pieces:
        draws = jnp.exp(jax.random.uniform(jax.random.fold_in(own, axis_at), (parts,), jnp.float32, smallest / len(pieces), largest / len(pieces)))
        factor_of = factor_of * jnp.repeat(draws, dims[axis_at] // parts).reshape([-1 if axis == axis_at else 1 for axis in range(len(dims))])
    return factor_of


def gaussian(own_key, extent, width, most, pieces=(), kind=jnp.bfloat16):
    level = block_levels(own_key, extent, pieces, -0.22, 0.18) if pieces else 1.0
    result = jax.random.normal(own_key, extent, jnp.float32) * width * level
    return jnp.minimum(jnp.maximum(result, -most), most).astype(kind)


def setup_inputs(seed: int = 0) -> dict:
    arg_keys = jax.random.split(jax.random.key(seed), 8)
    query_branch = gaussian(arg_keys[0], (SEQ, D), 1.0, 6.0, ((0, 16), (1, 8)))
    key_raw = gaussian(arg_keys[1], (SEQ, D), 1.0, 6.0, ((0, 16), (1, 8)))
    value_branch = gaussian(arg_keys[2], (SEQ, D), 1.0, 6.0, ((0, 16), (1, 8)))
    conv_out = gaussian(arg_keys[3], (SEQ, D), 1.0, 6.0, ((0, 16), (1, 8)))
    out_grad = draw_out_grad(jax.random.fold_in(arg_keys[7], 71), 0)
    long_filter = gaussian(arg_keys[5], (SEQ, D), SEQ ** -0.5, 0.09375, ((0, 16), (1, 8)))
    short_filter = gaussian(arg_keys[6], (TAPS, D), 0.6, 3.0, ((1, 8),), jnp.float32)
    return dict(query_branch=query_branch, key_raw=key_raw, value_branch=value_branch, conv_out=conv_out, out_grad=out_grad, long_filter=long_filter, short_filter=short_filter)


def reference(query_branch, key_raw, value_branch, conv_out, out_grad, long_filter, short_filter):
    weights = short_filter.astype(jnp.float32)
    padded_key = jnp.pad(key_raw.astype(jnp.float32), ((TAPS - 1, 0), (0, 0)))
    key_conv = jnp.zeros((SEQ, D), jnp.float32)
    for shift_tap in range(TAPS):
        key_conv = key_conv + weights[shift_tap] * padded_key[TAPS - 1 - shift_tap:TAPS - 1 - shift_tap + SEQ]
    value_wide = value_branch.astype(jnp.float32)
    gated = (key_conv * value_wide).astype(jnp.bfloat16)
    grad_wide = out_grad.astype(jnp.float32)
    query_grad = (grad_wide * conv_out.astype(jnp.float32)).astype(jnp.bfloat16)
    conv_grad = (grad_wide * query_branch.astype(jnp.float32)).astype(jnp.bfloat16)
    length = 2 * SEQ
    grad_spec = jnp.fft.rfft(conv_grad.astype(jnp.float32), n=length, axis=0)
    filter_spec = jnp.fft.rfft(long_filter.astype(jnp.float32), n=length, axis=0)
    gated_spec = jnp.fft.rfft(gated.astype(jnp.float32), n=length, axis=0)
    gated_grad = jnp.fft.irfft(jnp.conj(filter_spec) * grad_spec, n=length, axis=0)[:SEQ].astype(jnp.float32)
    lag_grad = jnp.fft.irfft(jnp.conj(gated_spec) * grad_spec, n=length, axis=0)[:SEQ].astype(jnp.float32)
    value_grad = (gated_grad * key_conv).astype(jnp.bfloat16)
    key_grad = gated_grad * value_wide
    padded_grad = jnp.pad(key_grad, ((0, TAPS - 1), (0, 0)))
    raw_total = jnp.zeros((SEQ, D), jnp.float32)
    for shift_tap in range(TAPS):
        raw_total = raw_total + weights[shift_tap] * padded_grad[shift_tap:shift_tap + SEQ]
    key_raw_grad = raw_total.astype(jnp.bfloat16)
    short_grad = jnp.stack([lax.optimization_barrier(jnp.sum(key_grad * padded_key[TAPS - 1 - shift_tap:TAPS - 1 - shift_tap + SEQ], axis=0)) for shift_tap in range(TAPS)])
    squares_mean = jnp.mean(lag_grad * lag_grad)
    scale_factor = lax.rsqrt(squares_mean + 1e-06)
    filter_grad = lag_grad * scale_factor
    return (query_grad, key_raw_grad, value_grad, filter_grad, short_grad)
```

```python
import functools

import jax
import jax.numpy as jnp
import ml_dtypes
import numpy as np
from jax import lax
from jax.experimental import pallas as pl
from jax.experimental.pallas import tpu as pltpu
from jax.sharding import PartitionSpec as P

MESH = pl.DeviceIdType.MESH
F32, BF16 = jnp.float32, jnp.bfloat16
ROWS, WIDTH, LANES, CHIPS, BLOCKS = 256, 1024, 128, 8, 16
TAPS = 3
STEPS = ((0, 1), (1, 0), (0, 3), (1, 1), (0, 2), (1, 3), (1, 2))


def tables():
    length = 2 * ROWS
    rows = np.arange(length)
    freq = np.where(rows <= ROWS, rows, rows - ROWS)
    angle = (freq[:, None] * np.arange(ROWS)[None, :] % length) * (np.pi / ROWS)
    forward = np.where((rows <= ROWS)[:, None], np.cos(angle), -np.sin(angle))
    weight = np.where((freq == 0) | (freq == ROWS), 1.0, 2.0) / length
    inverse = forward.T * weight[None, :]

    def pair(table):
        upper = table.astype(ml_dtypes.bfloat16)
        lower = (table - upper.astype(np.float64)).astype(ml_dtypes.bfloat16)
        return np.concatenate([upper, lower], axis=0)

    return pair(forward), pair(inverse)


def lanes(index):
    return pl.ds(pl.multiple_of(index * LANES, LANES), LANES)


def kernel(
    qb_hbm, kr_hbm, vb_hbm, co_hbm, og_hbm, lf_hbm, taps_ref, fwd_hbm, inv_hbm,
    qg_hbm, krg_hbm, vg_hbm, fg_hbm, sg_ref,
    qb, kr, vb, co, og, lf, fwd, inv,
    cg, gated, ext, conv, halo, land_g, land_a, spec_g, sum_g, spec_a, dif_a,
    prod_hi, prod_lo, back, ret, keyg, tail, qg, krg, vg, fg,
    part, part_land, short, squares, squares_land, total, total_land,
    in_sem, out_sem, halo_sem, tail_sem,
    gs_sem, gr_sem, fs_sem, fr_sem, as_sem, ar_sem, own_sem, rs_sem, rr_sem,
    ps_sem, pr_sem, bs_sem, br_sem, s1s_sem, s1r_sem, s2s_sem, s2r_sem,
):
    me = lax.axis_index("ctx")
    group = lax.axis_index("ch")
    chip, core = me // 2, lax.rem(me, 2)
    sibling = chip * 2 + 1 - core
    chip_x, chip_y = chip // 4, lax.rem(chip, 4)

    def chip_at(dx, dy):
        return lax.rem(chip_x + dx, 2) * 4 + lax.rem(chip_y + dy, 4)

    dests = [chip_at(dx, dy) for dx, dy in STEPS]
    sources = [chip_at(2 - dx, 4 - dy) for dx, dy in STEPS]

    def remote(src, dst, send, recv, ctx):
        return pltpu.make_async_remote_copy(
            src_ref=src, dst_ref=dst, send_sem=send, recv_sem=recv,
            device_id={"ctx": ctx}, device_id_type=MESH,
        )

    def arrived(ref, sem):
        pltpu.make_async_copy(ref, ref, sem).wait()

    loads = [
        pltpu.make_async_copy(src, dst, in_sem.at[n])
        for n, (src, dst) in enumerate(
            ((og_hbm, og), (qb_hbm, qb), (kr_hbm, kr), (lf_hbm, lf), (vb_hbm, vb),
             (fwd_hbm, fwd), (co_hbm, co), (inv_hbm, inv))
        )
    ]
    for load in loads:
        load.start()
    og_in, qb_in, kr_in, lf_in, vb_in, fwd_in, co_in, inv_in = loads

    barrier = pltpu.get_barrier_semaphore()
    for step in range(1, BLOCKS):
        pl.semaphore_signal(
            barrier, inc=1, device_id={"ctx": lax.rem(me + step, BLOCKS)}, device_id_type=MESH
        )
    for step in range(1, 8):
        pl.semaphore_signal(
            barrier, inc=1, device_id={"ch": lax.rem(group + step, 8)}, device_id_type=MESH
        )

    og_in.wait()
    qb_in.wait()

    def make_grad(p, carry):
        at = lanes(p)
        cg[:, at] = (og[:, at].astype(F32) * qb[:, at].astype(F32)).astype(BF16)
        return carry

    lax.fori_loop(0, CHIPS, make_grad, 0)
    kr_in.wait()
    lf_in.wait()
    pl.semaphore_wait(barrier, BLOCKS - 1 + 7)

    def halo_copy():
        return remote(
            kr.at[pl.ds(ROWS - 16, 16)], halo, halo_sem.at[0], halo_sem.at[1],
            lax.rem(me + 1, BLOCKS),
        )

    @pl.when(me < BLOCKS - 1)
    def _():
        halo_copy().start()

    mine = lanes(core)
    own_grad = remote(
        cg.at[:, lanes(chip)], land_g.at[chip, :, mine], gs_sem.at[7], fr_sem.at[chip], sibling
    )
    own_grad.start()
    grad_sends = [own_grad]
    for n, p in enumerate(dests):
        copy = remote(
            cg.at[:, lanes(p)], land_g.at[chip, :, mine], gs_sem.at[n], gr_sem.at[chip],
            p * 2 + core,
        )
        copy.start()
        grad_sends.append(copy)
    keep_grad = pltpu.make_async_copy(
        cg.at[:, lanes(chip)], land_g.at[chip, :, mine], own_sem.at[0]
    )
    keep_grad.start()

    def send_to_core(block, goal, first):
        copies = []
        for n, p in enumerate(dests):
            copy = remote(
                block.at[:, lanes(p)], land_a.at[chip, :, mine], as_sem.at[first + n],
                ar_sem.at[me], p * 2 + goal,
            )
            copy.start()
            copies.append(copy)

        @pl.when(core == goal)
        def _():
            pltpu.make_async_copy(
                block.at[:, lanes(chip)], land_a.at[chip, :, mine], own_sem.at[1]
            ).start()

        @pl.when(core != goal)
        def _():
            remote(
                block.at[:, lanes(chip)], land_a.at[chip, :, mine], as_sem.at[first + 7],
                ar_sem.at[me], sibling,
            ).start()

        return copies

    filter_sends = send_to_core(lf, 0, 0)

    vb_in.wait()

    @pl.when(me > 0)
    def _():
        arrived(halo, halo_sem.at[1])
        ext[0:8, :] = halo[...].astype(F32)[8:16]

    @pl.when(me == 0)
    def _():
        ext[0:8, :] = jnp.zeros((8, WIDTH), F32)

    def make_gated(p, carry):
        at = lanes(p)
        ext[8:, at] = kr[:, at].astype(F32)
        value = jnp.zeros((ROWS, LANES), F32)
        for j in range(TAPS):
            value = value + taps_ref[j : j + 1, at] * ext[8 - j : 8 - j + ROWS, at]
        conv[:, at] = value
        gated[:, at] = (value * vb[:, at].astype(F32)).astype(BF16)
        return carry

    lax.fori_loop(0, CHIPS, make_gated, 0)
    gated_sends = send_to_core(gated, 1, 8)

    co_in.wait()

    def make_query(p, carry):
        at = lanes(p)
        qg[:, at] = (og[:, at].astype(F32) * co[:, at].astype(F32)).astype(BF16)
        return carry

    lax.fori_loop(0, CHIPS, make_query, 0)
    qg_out = pltpu.make_async_copy(qg, qg_hbm, out_sem.at[0])
    qg_out.start()

    fwd_in.wait()

    def transform(block):
        upper = jnp.dot(fwd[: 2 * ROWS], block, preferred_element_type=F32)
        return upper + jnp.dot(fwd[2 * ROWS :], block, preferred_element_type=F32)

    other = lanes(1 - core)

    def grad_spectrum(source):
        arrived(land_g.at[source, :, other], fr_sem.at[source])
        spec_g[source] = transform(land_g[source])

    spec_g[CHIPS] = jnp.zeros((2 * ROWS, 2 * LANES), F32)
    keep_grad.wait()
    waiting = chip
    forwards = []
    for n, source in enumerate(sources):
        block = land_g.at[source, :, mine]
        arrived(block, gr_sem.at[source])
        copy = remote(block, block, fs_sem.at[n], fr_sem.at[source], sibling)
        copy.start()
        forwards.append(copy)
        grad_spectrum(waiting)
        waiting = source
    grad_spectrum(waiting)

    def join(m, carry):
        even = (lax.broadcasted_iota(jnp.int32, (2 * ROWS, LANES), 0) % 2) == 0
        first, second = spec_g[m, :, :LANES], spec_g[m, :, LANES:]
        third = spec_g[m + 1, :, :LANES]
        first = first + jnp.where(even, second, -second)
        second = second + jnp.where(even, third, -third)
        spec_g[m, :, :LANES] = first
        spec_g[m, :, LANES:] = second
        sum_g[m, :, :LANES] = first[:ROWS] + first[ROWS:]
        sum_g[m, :, LANES:] = second[:ROWS] + second[ROWS:]
        return carry

    lax.fori_loop(0, CHIPS, join, 0)

    def a_spectrum(source):
        result = transform(land_a[source])
        spec_a[source] = result
        dif_a[source] = result[:ROWS] - result[ROWS:]

    arrived(land_a.at[chip, :, mine], own_sem.at[1])
    arrived(land_a.at[chip, :, other], ar_sem.at[sibling])
    a_spectrum(chip)
    for source in sources:
        arrived(land_a.at[source, :, :LANES], ar_sem.at[source * 2])
        arrived(land_a.at[source, :, LANES:], ar_sem.at[source * 2 + 1])
        a_spectrum(source)

    def products(chunk, carry):
        for base in range(0, BLOCKS, 4):
            halves = []
            for sub in range(2):
                row = pl.multiple_of(chunk * 16 + sub * 8, 8)
                re_at, im_at = pl.ds(row, 8), pl.ds(pl.multiple_of(row + ROWS, 8), 8)
                real = [None] * 4
                both = [None] * 4
                cross = [None] * 4
                held = []
                for m in range(base, BLOCKS):
                    at = slice((m % 2) * LANES, (m % 2 + 1) * LANES)
                    g_re, g_im = spec_g[m // 2, re_at, at], spec_g[m // 2, im_at, at]
                    g_sum = sum_g[m // 2, re_at, at]
                    j = m - base
                    at = slice((j % 2) * LANES, (j % 2 + 1) * LANES)
                    held.append(
                        (spec_a[j // 2, re_at, at], spec_a[j // 2, im_at, at], dif_a[j // 2, re_at, at])
                    )
                    for u in range(min(4, j + 1)):
                        a_re, a_im, a_dif = held[j - u]
                        terms = (a_re * g_re, a_im * g_im, a_dif * g_sum)
                        for sums, term in zip((real, both, cross), terms):
                            sums[u] = term if sums[u] is None else sums[u] + term
                edge = (lax.broadcasted_iota(jnp.int32, (8, LANES), 0) + row) == 0
                halves.append(
                    [
                        (
                            jnp.where(edge, real[u], real[u] + both[u]),
                            jnp.where(edge, both[u], cross[u] - real[u] + both[u]),
                        )
                        for u in range(4)
                    ]
                )
            start = pl.multiple_of(chunk * 16, 16)
            for u in range(4):
                at = slice((base + u) * LANES, (base + u + 1) * LANES)
                for part_at, offset in ((0, 0), (1, ROWS)):
                    value = jnp.concatenate([halves[0][u][part_at], halves[1][u][part_at]], axis=0)
                    upper = value.astype(BF16)
                    rows_at = pl.ds(pl.multiple_of(start + offset, 16), 16)
                    prod_hi[rows_at, at] = upper
                    prod_lo[rows_at, at] = (value - upper.astype(F32)).astype(BF16)
        return carry

    lax.fori_loop(0, ROWS // 16, products, 0)

    inv_in.wait()
    squares[...] = jnp.zeros((8, LANES), F32)

    def restore(p):
        at = pl.ds(pl.multiple_of(p * 2 * LANES, 2 * LANES), 2 * LANES)
        upper = prod_hi[:, at]
        both = jnp.dot(inv[...], upper, preferred_element_type=F32)
        result = both[:ROWS] + both[ROWS:]
        result = result + jnp.dot(inv[:ROWS], prod_lo[:, at], preferred_element_type=F32)
        back[p] = result.astype(BF16)
        square = result[:, :LANES] * result[:, :LANES] + result[:, LANES:] * result[:, LANES:]
        squares[...] += jnp.sum(square.reshape(ROWS // 8, 8, LANES), axis=0)

    returns = []

    def give_back(n, p, half):
        copy = remote(
            back.at[p, :, half * LANES : (half + 1) * LANES], ret.at[core, :, lanes(chip)],
            rs_sem.at[n * 2 + half], rr_sem.at[core * 8 + chip], p * 2 + half,
        )
        copy.start()
        returns.append(copy)

    for n, p in enumerate(dests):
        restore(p)
        give_back(n, p, 0)
        give_back(n, p, 1)
    restore(chip)
    keep_back = pltpu.make_async_copy(
        back.at[chip, :, mine], ret.at[core, :, lanes(chip)], own_sem.at[0]
    )
    keep_back.start()
    own_back = remote(
        back.at[chip, :, other], ret.at[core, :, lanes(chip)],
        rs_sem.at[14], rr_sem.at[core * 8 + chip], sibling,
    )
    own_back.start()

    def squares_copy(step):
        return remote(
            squares, squares_land.at[chip], s1s_sem.at[step], s1r_sem.at[chip],
            lax.rem(me + step, BLOCKS),
        )

    @pl.when(core == 1)
    def _():
        for step in range(1, BLOCKS):
            squares_copy(step).start()
        squares_land[chip] = squares[...]

    part[...] = jnp.zeros((8, WIDTH), F32)
    keep_back.wait()

    def branch(source):
        at = lanes(source)
        wide = ret[0, :, at].astype(F32)
        vg[:, at] = (wide * conv[:, at]).astype(BF16)
        key = wide * vb[:, at].astype(F32)
        keyg[0:ROWS, at] = key
        for j in range(TAPS):
            part[j : j + 1, at] = jnp.sum(key * ext[8 - j : 8 - j + ROWS, at], axis=0, keepdims=True)

    @pl.when(core == 1)
    def _():
        arrived(ret.at[0, :, lanes(chip)], rr_sem.at[chip])

    branch(chip)
    for source in sources:
        arrived(ret.at[0, :, lanes(source)], rr_sem.at[source])
        branch(source)
    vg_out = pltpu.make_async_copy(vg, vg_hbm, out_sem.at[1])
    vg_out.start()

    def tail_copy():
        return remote(
            keyg.at[pl.ds(0, 8)], tail, tail_sem.at[0], tail_sem.at[1],
            lax.rem(me + BLOCKS - 1, BLOCKS),
        )

    @pl.when(me > 0)
    def _():
        tail_copy().start()

    part_sends = []
    for n, p in enumerate(dests):
        copy = remote(
            part.at[:, lanes(p)], part_land.at[me], ps_sem.at[n], pr_sem.at[me], p * 2
        )
        copy.start()
        part_sends.append(copy)

    def part_copy():
        return remote(part.at[:, lanes(chip)], part_land.at[me], ps_sem.at[7], pr_sem.at[me], sibling)

    @pl.when(core == 1)
    def _():
        part_copy().start()

    @pl.when(core == 0)
    def _():
        part_land[me] = part[:, lanes(chip)]

    for source in sources:
        arrived(squares_land.at[source], s1r_sem.at[source])

    @pl.when(core == 0)
    def _():
        arrived(squares_land.at[chip], s1r_sem.at[chip])

    total[...] = jnp.sum(squares_land[...], axis=0)
    total_sends = []
    for step in range(1, 8):
        copy = pltpu.make_async_remote_copy(
            src_ref=total, dst_ref=total_land.at[group], send_sem=s2s_sem.at[step],
            recv_sem=s2r_sem.at[group], device_id={"ch": lax.rem(group + step, 8)},
            device_id_type=MESH,
        )
        copy.start()
        total_sends.append(copy)
    total_land[group] = total[...]

    @pl.when(me < BLOCKS - 1)
    def _():
        arrived(tail, tail_sem.at[1])
        keyg[ROWS : ROWS + 8, :] = tail[...]

    @pl.when(me == BLOCKS - 1)
    def _():
        keyg[ROWS : ROWS + 8, :] = jnp.zeros((8, WIDTH), F32)

    def make_raw(p, carry):
        at = lanes(p)
        value = jnp.zeros((ROWS, LANES), F32)
        for j in range(TAPS):
            value = value + taps_ref[j : j + 1, at] * keyg[j : j + ROWS, at]
        krg[:, at] = value.astype(BF16)
        return carry

    lax.fori_loop(0, CHIPS, make_raw, 0)
    krg_out = pltpu.make_async_copy(krg, krg_hbm, out_sem.at[2])
    krg_out.start()

    def short_copy(step):
        return remote(
            short.at[:, lanes(chip)], short.at[:, lanes(chip)], bs_sem.at[step], br_sem.at[chip],
            lax.rem(me + step, BLOCKS),
        )

    @pl.when(core == 0)
    def _():
        for source in sources:
            arrived(part_land.at[source * 2], pr_sem.at[source * 2])
            arrived(part_land.at[source * 2 + 1], pr_sem.at[source * 2 + 1])
        arrived(part_land.at[sibling], pr_sem.at[sibling])
        short[:, lanes(chip)] = jnp.sum(part_land[...], axis=0)
        for step in range(1, BLOCKS):
            short_copy(step).start()

    for step in range(1, 8):
        source = lax.rem(group + 8 - step, 8)
        arrived(total_land.at[source], s2r_sem.at[source])
    everything = jnp.sum(jnp.sum(total_land[...], axis=0), axis=(0, 1), keepdims=True)
    scale = lax.rsqrt(everything / float(4096 * 8192) + 1e-06)

    fg_outs = []

    def scaled(n, source):
        at = lanes(source)
        fg[:, at] = ret[1, :, at].astype(F32) * scale
        copy = pltpu.make_async_copy(fg.at[:, at], fg_hbm.at[:, at], out_sem.at[3 + n])
        copy.start()
        fg_outs.append(copy)

    @pl.when(core == 0)
    def _():
        arrived(ret.at[1, :, lanes(chip)], rr_sem.at[8 + chip])

    scaled(7, chip)
    for n, source in enumerate(sources):
        arrived(ret.at[1, :, lanes(source)], rr_sem.at[8 + source])
        scaled(n, source)

    for source in sources:
        arrived(short.at[:, lanes(source)], br_sem.at[source])

    @pl.when(core == 1)
    def _():
        arrived(short.at[:, lanes(chip)], br_sem.at[chip])

    sg_ref[...] = short[0:TAPS, :]

    for copy in grad_sends + filter_sends + gated_sends + forwards + returns + [own_back]:
        copy.wait_send()
    for copy in part_sends + total_sends:
        copy.wait_send()

    @pl.when(me < BLOCKS - 1)
    def _():
        halo_copy().wait_send()

    @pl.when(me > 0)
    def _():
        tail_copy().wait_send()

    @pl.when(core == 0)
    def _():
        for step in range(1, BLOCKS):
            short_copy(step).wait_send()
        remote(
            gated.at[:, lanes(chip)], land_a.at[chip, :, mine], as_sem.at[15], ar_sem.at[me], sibling
        ).wait_send()

    @pl.when(core == 1)
    def _():
        part_copy().wait_send()
        for step in range(1, BLOCKS):
            squares_copy(step).wait_send()
        remote(
            lf.at[:, lanes(chip)], land_a.at[chip, :, mine], as_sem.at[7], ar_sem.at[me], sibling
        ).wait_send()

    for copy in [qg_out, vg_out, krg_out] + fg_outs:
        copy.wait()


def per_device(query_branch, key_raw, value_branch, conv_out, out_grad, long_filter, short_filter):
    forward, inverse = tables()
    anywhere = pl.BlockSpec(memory_space=pl.ANY)
    in_vmem = pl.BlockSpec(memory_space=pltpu.VMEM)
    block = jax.ShapeDtypeStruct((ROWS, WIDTH), BF16)
    dma = pltpu.SemaphoreType.DMA
    vmem = pltpu.VMEM
    return pl.pallas_call(
        kernel,
        out_shape=(
            block, block, block,
            jax.ShapeDtypeStruct((ROWS, WIDTH), F32),
            jax.ShapeDtypeStruct((TAPS, WIDTH), F32),
        ),
        in_specs=[anywhere] * 6 + [in_vmem] + [anywhere] * 2,
        out_specs=(anywhere, anywhere, anywhere, anywhere, in_vmem),
        scratch_shapes=[
            *[vmem((ROWS, WIDTH), BF16)] * 6,
            vmem((4 * ROWS, ROWS), BF16),
            vmem((2 * ROWS, 2 * ROWS), BF16),
            vmem((ROWS, WIDTH), BF16),
            vmem((ROWS, WIDTH), BF16),
            vmem((ROWS + 8, WIDTH), F32),
            vmem((ROWS, WIDTH), F32),
            vmem((16, WIDTH), BF16),
            vmem((CHIPS, ROWS, 2 * LANES), BF16),
            vmem((CHIPS, ROWS, 2 * LANES), BF16),
            vmem((CHIPS + 1, 2 * ROWS, 2 * LANES), F32),
            vmem((CHIPS, ROWS, 2 * LANES), F32),
            vmem((CHIPS, 2 * ROWS, 2 * LANES), F32),
            vmem((CHIPS, ROWS, 2 * LANES), F32),
            vmem((2 * ROWS, BLOCKS * LANES), BF16),
            vmem((2 * ROWS, BLOCKS * LANES), BF16),
            vmem((CHIPS, ROWS, 2 * LANES), BF16),
            vmem((2, ROWS, WIDTH), BF16),
            vmem((ROWS + 8, WIDTH), F32),
            vmem((8, WIDTH), F32),
            *[vmem((ROWS, WIDTH), BF16)] * 3,
            vmem((ROWS, WIDTH), F32),
            vmem((8, WIDTH), F32),
            vmem((BLOCKS, 8, LANES), F32),
            vmem((8, WIDTH), F32),
            vmem((8, LANES), F32),
            vmem((CHIPS, 8, LANES), F32),
            vmem((8, LANES), F32),
            vmem((8, 8, LANES), F32),
            dma((8,)), dma((11,)), dma((2,)), dma((2,)),
            dma((8,)), dma((8,)), dma((8,)), dma((8,)), dma((16,)), dma((16,)), dma((2,)),
            dma((16,)), dma((16,)),
            dma((8,)), dma((16,)), dma((16,)), dma((8,)),
            dma((16,)), dma((8,)), dma((8,)), dma((8,)),
        ],
        compiler_params=pltpu.CompilerParams(
            collective_id=0, has_side_effects=True, vmem_limit_bytes=56 * 2**20
        ),
        cost_estimate=pl.CostEstimate(flops=6 * 10**9, bytes_accessed=7 * 2**20, transcendentals=0),
    )(
        query_branch, key_raw, value_branch, conv_out, out_grad, long_filter, short_filter,
        jnp.asarray(forward), jnp.asarray(inverse),
    )


def solution(mesh):
    both, taps = P("ctx", "ch"), P(None, "ch")
    return jax.shard_map(
        per_device,
        mesh=mesh,
        in_specs=(both,) * 6 + (taps,),
        out_specs=(both,) * 4 + (taps,),
        check_vma=False,
    )
```

```python
import functools

import jax
import jax.numpy as jnp
import ml_dtypes
import numpy as np
from jax import lax
from jax.experimental import pallas as pl
from jax.experimental.pallas import tpu as pltpu
from jax.sharding import PartitionSpec as P

MESH = pl.DeviceIdType.MESH
F32, BF16 = jnp.float32, jnp.bfloat16
ROWS, WIDTH, LANES, CHIPS, BLOCKS = 256, 1024, 128, 8, 16
TAPS = 3
FINISH_PARTS = 4
FIRST = 4
AHEAD = 4


def tables():
    length = 2 * ROWS
    rows = np.arange(length)
    freq = np.where(rows <= ROWS, rows, rows - ROWS)
    angle = (freq[:, None] * np.arange(ROWS)[None, :] % length) * (np.pi / ROWS)
    forward = np.where((rows <= ROWS)[:, None], np.cos(angle), -np.sin(angle))
    weight = np.where((freq == 0) | (freq == ROWS), 1.0, 2.0) / length
    inverse = forward.T * weight[None, :]

    def pair(table):
        upper = table.astype(ml_dtypes.bfloat16)
        lower = (table - upper.astype(np.float64)).astype(ml_dtypes.bfloat16)
        return np.concatenate([upper, lower], axis=0)

    return pair(forward), pair(inverse)


def lanes(index):
    return pl.ds(pl.multiple_of(index * LANES, LANES), LANES)


def kernel(
    qb_hbm, kr_hbm, vb_hbm, co_hbm, og_hbm, lf_hbm, taps_ref, fwd_hbm, inv_hbm,
    qg, krg, vg, lag, total_all, short,
    qb, kr, vb, co, og, lf, fwd, inv,
    cg, gated, ext, conv, halo, land, spec_g, sum_g, spec_a, dif_a,
    prod_hi, prod_lo, back, ret, keyg, tail,
    part, pack, pack_land, half_short, half_land, squares, squares_land, total, total_land,
    in_sem, halo_sem, tail_sem, send_sem, come_sem, pass_sem, other_sem, own_sem, rs_sem, rr_sem,
    pack_sem, bs_sem, br_sem, s1s_sem, s1r_sem, s2s_sem, s2r_sem,
):
    me = lax.axis_index("ctx")
    group = lax.axis_index("ch")
    chip, core = me // 2, lax.rem(me, 2)
    sibling = chip * 2 + 1 - core
    chip_x, chip_y = chip // 4, lax.rem(chip, 4)

    def chip_at(step, sign):
        dx, dy = lax.rem(step, 2), step // 2
        return lax.rem(chip_x + dx, 2) * 4 + lax.rem(chip_y + 4 + sign * dy, 4)

    dests = [chip_at(step, 1) for step in range(1, CHIPS)]
    sources = [chip_at(step, -1) for step in range(1, CHIPS)]
    mine, other = lanes(core), lanes(1 - core)

    def remote(src, dst, send, recv, ctx):
        return pltpu.make_async_remote_copy(
            src_ref=src, dst_ref=dst, send_sem=send, recv_sem=recv,
            device_id={"ctx": ctx}, device_id_type=MESH,
        )

    def arrived(ref, sem):
        pltpu.make_async_copy(ref, ref, sem).wait()

    loads = [
        pltpu.make_async_copy(src, dst, in_sem.at[n])
        for n, (src, dst) in enumerate(
            ((og_hbm, og), (qb_hbm, qb), (kr_hbm, kr), (lf_hbm, lf), (vb_hbm, vb),
             (fwd_hbm, fwd), (co_hbm, co), (inv_hbm, inv))
        )
    ]
    for load in loads:
        load.start()
    og_in, qb_in, kr_in, lf_in, vb_in, fwd_in, co_in, inv_in = loads

    barrier = pltpu.get_barrier_semaphore()
    for step in range(1, BLOCKS):
        pl.semaphore_signal(
            barrier, inc=1, device_id={"ctx": lax.rem(me + step, BLOCKS)}, device_id_type=MESH
        )
    for step in range(1, 8):
        pl.semaphore_signal(
            barrier, inc=1, device_id={"ch": lax.rem(group + step, 8)}, device_id_type=MESH
        )

    og_in.wait()
    qb_in.wait()

    def make_grad(p, carry):
        at = lanes(p)
        cg[:, at] = (og[:, at].astype(F32) * qb[:, at].astype(F32)).astype(BF16)
        return carry

    lax.fori_loop(0, CHIPS, make_grad, 0)
    kr_in.wait()
    lf_in.wait()
    pl.semaphore_wait(barrier, BLOCKS - 1 + 7)

    def halo_copy():
        return remote(
            kr.at[pl.ds(ROWS - 16, 16)], halo, halo_sem.at[0], halo_sem.at[1],
            lax.rem(me + 1, BLOCKS),
        )

    @pl.when(me < BLOCKS - 1)
    def _():
        halo_copy().start()

    def send_out(kind, block):
        copies = []
        for n, p in enumerate([chip] + dests):
            own = n == 0
            copies.append(
                remote(
                    block.at[:, lanes(p)], land.at[kind, chip, :, mine], send_sem.at[kind, n],
                    other_sem.at[kind, chip] if own else come_sem.at[kind, chip],
                    sibling if own else p * 2 + core,
                )
            )
            copies[-1].start()
        keep = pltpu.make_async_copy(
            block.at[:, lanes(chip)], land.at[kind, chip, :, mine], own_sem.at[kind]
        )
        keep.start()
        return copies, keep

    grad_sends, grad_keep = send_out(0, cg)
    filter_sends, filter_keep = send_out(1, lf)

    vb_in.wait()

    @pl.when(me > 0)
    def _():
        arrived(halo, halo_sem.at[1])
        ext[0:8, :] = halo[...].astype(F32)[8:16]

    @pl.when(me == 0)
    def _():
        ext[0:8, :] = jnp.zeros((8, WIDTH), F32)

    def make_gated(p, carry):
        at = lanes(p)
        ext[8:, at] = kr[:, at].astype(F32)
        value = jnp.zeros((ROWS, LANES), F32)
        for j in range(TAPS):
            value = value + taps_ref[j : j + 1, at] * ext[8 - j : 8 - j + ROWS, at]
        conv[:, at] = value
        gated[:, at] = (value * vb[:, at].astype(F32)).astype(BF16)
        return carry

    lax.fori_loop(0, CHIPS, make_gated, 0)
    gated_sends, gated_keep = send_out(2, gated)
    co_in.wait()

    def make_query(p, carry):
        at = lanes(p)
        qg[:, at] = (og[:, at].astype(F32) * co[:, at].astype(F32)).astype(BF16)
        return carry

    lax.fori_loop(0, CHIPS, make_query, 0)

    fwd_in.wait()

    def transform(block):
        upper = jnp.dot(fwd[: 2 * ROWS], block, preferred_element_type=F32)
        return upper + jnp.dot(fwd[2 * ROWS :], block, preferred_element_type=F32)

    def spectra(kind, keep, put):
        def pair(source):
            arrived(land.at[kind, source, :, other], other_sem.at[kind, source])
            put(source, transform(land[kind, source]))

        def handed(step):
            source = chip_at(step, -1)
            block = land.at[kind, source, :, mine]
            return remote(
                block, block, pass_sem.at[kind, step], other_sem.at[kind, source], sibling
            )

        def hand(step):
            source = chip_at(step, -1)
            arrived(land.at[kind, source, :, mine], come_sem.at[kind, source])
            handed(step).start()

        def turn(step, carry):
            @pl.when(step < CHIPS)
            def _():
                hand(step)

            pair(chip_at(step - AHEAD, -1))
            return carry

        keep.wait()
        for step in range(1, AHEAD):
            hand(step)
        lax.fori_loop(AHEAD, CHIPS + AHEAD, turn, 0)
        return [handed(step) for step in range(1, CHIPS)]

    def put_grad(source, value):
        spec_g[source] = value

    def put_other(source, value):
        spec_a[source] = value
        dif_a[source] = value[:ROWS] - value[ROWS:]

    handed = spectra(0, grad_keep, put_grad)
    spec_g[CHIPS] = jnp.zeros((2 * ROWS, 2 * LANES), F32)

    def join_from(first):
        def join(m, carry):
            even = (lax.broadcasted_iota(jnp.int32, (2 * ROWS, LANES), 0) % 2) == 0
            for n in range(2):
                now, later = first + n, first + n + 1
                a = spec_g[m + now // 2, :, now % 2 * LANES : (now % 2 + 1) * LANES]
                b = spec_g[m + later // 2, :, later % 2 * LANES : (later % 2 + 1) * LANES]
                value = a + jnp.where(even, b, -b)
                at = slice(n * LANES, (n + 1) * LANES)
                spec_g[m, :, at] = value
                sum_g[m, :, at] = value[:ROWS] + value[ROWS:]
            return carry

        lax.fori_loop(0, CHIPS, join, 0)

    @pl.when(core == 0)
    def _():
        join_from(0)

    @pl.when(core == 1)
    def _():
        join_from(1)

    def products(chunk, carry):
        for base in (0, 8):
            halves = []
            for sub in range(2):
                row = pl.multiple_of(chunk * 16 + sub * 8, 8)
                re_at, im_at = pl.ds(row, 8), pl.ds(pl.multiple_of(row + ROWS, 8), 8)
                real, both, cross, held = [None] * 4, [None] * 4, [None] * 4, []
                for m in range(base, BLOCKS):
                    at = slice((m % 2) * LANES, (m % 2 + 1) * LANES)
                    g_re, g_im = spec_g[m // 2, re_at, at], spec_g[m // 2, im_at, at]
                    g_sum = sum_g[m // 2, re_at, at]
                    j = m - base
                    at = slice((j % 2) * LANES, (j % 2 + 1) * LANES)
                    held.append(
                        (spec_a[j // 2, re_at, at], spec_a[j // 2, im_at, at], dif_a[j // 2, re_at, at])
                    )
                    for u in range(min(4, j // 2 + 1)):
                        a_re, a_im, a_dif = held[j - 2 * u]
                        terms = (a_re * g_re, a_im * g_im, a_dif * g_sum)
                        for sums, term in zip((real, both, cross), terms):
                            sums[u] = term if sums[u] is None else sums[u] + term
                edge = (lax.broadcasted_iota(jnp.int32, (8, LANES), 0) + row) == 0
                halves.append(
                    [
                        (
                            jnp.where(edge, real[u], real[u] + both[u]),
                            jnp.where(edge, both[u], cross[u] - real[u] + both[u]),
                        )
                        for u in range(4)
                    ]
                )
            start = pl.multiple_of(chunk * 16, 16)
            for u in range(4):
                at = slice((base // 2 + u) * LANES, (base // 2 + u + 1) * LANES)
                for which, offset in ((0, 0), (1, ROWS)):
                    value = jnp.concatenate([halves[0][u][which], halves[1][u][which]], axis=0)
                    upper = value.astype(BF16)
                    rows_at = pl.ds(pl.multiple_of(start + offset, 16), 16)
                    prod_hi[rows_at, at] = upper
                    prod_lo[rows_at, at] = (value - upper.astype(F32)).astype(BF16)
        return carry

    def restore(kind):
        twice = jnp.dot(inv[...], prod_hi[...], preferred_element_type=F32)
        result = twice[:ROWS] + twice[ROWS:]
        result = result + jnp.dot(inv[:ROWS], prod_lo[...], preferred_element_type=F32)
        for k in range(CHIPS // 2):
            back[kind, k] = result[:, k * 2 * LANES : (k + 1) * 2 * LANES].astype(BF16)
        if kind == 1:
            square = result * result
            square = sum(square[:, k * LANES : (k + 1) * LANES] for k in range(CHIPS))
            squares[...] = jnp.sum(square.reshape(ROWS // 8, 8, LANES), axis=0)

    def give_back(kind, n, p, goal):
        copy = remote(
            back.at[kind, p // 2, :, lanes(lax.rem(p, 2))], goal.at[:, lanes(chip)],
            rs_sem.at[kind, n], rr_sem.at[kind, chip], p * 2 + core,
        )
        copy.start()
        return copy

    def keep_back(kind, goal):
        copy = pltpu.make_async_copy(
            back.at[kind, chip // 2, :, lanes(lax.rem(chip, 2))], goal.at[:, lanes(chip)],
            own_sem.at[3 + kind],
        )
        copy.start()
        return copy

    handed = handed + spectra(1, filter_keep, put_other)
    lax.fori_loop(0, ROWS // 16, products, 0)
    inv_in.wait()
    restore(0)
    returns = [give_back(0, n, p, ret) for n, p in enumerate(dests)]
    ret_keep = keep_back(0, ret)

    handed = handed + spectra(2, gated_keep, put_other)
    lax.fori_loop(0, ROWS // 16, products, 0)
    restore(1)

    square_sends = []
    for step in range(1, BLOCKS):
        copy = remote(
            squares, squares_land.at[me], s1s_sem.at[step], s1r_sem.at[me],
            lax.rem(me + step, BLOCKS),
        )
        copy.start()
        square_sends.append(copy)
    squares_land[me] = squares[...]
    returns += [give_back(1, n, p, lag) for n, p in enumerate(dests[:FIRST])]
    lag_keep = keep_back(1, lag)

    part[...] = jnp.zeros((8, WIDTH), F32)

    def branch(source):
        at = lanes(source)
        wide = ret[:, at].astype(F32)
        vg[:, at] = (wide * conv[:, at]).astype(BF16)
        key = wide * vb[:, at].astype(F32)
        keyg[0:ROWS, at] = key
        for j in range(TAPS):
            part[j : j + 1, at] = jnp.sum(key * ext[8 - j : 8 - j + ROWS, at], axis=0, keepdims=True)

    def branch_turn(step, carry):
        source = chip_at(step, -1)
        arrived(ret.at[:, lanes(source)], rr_sem.at[0, source])
        branch(source)
        return carry

    ret_keep.wait()
    branch(chip)
    lax.fori_loop(1, CHIPS, branch_turn, 0)

    def tail_copy():
        return remote(
            keyg.at[pl.ds(0, 8)], tail, tail_sem.at[0], tail_sem.at[1],
            lax.rem(me + BLOCKS - 1, BLOCKS),
        )

    @pl.when(me > 0)
    def _():
        tail_copy().start()

    for p in range(CHIPS):
        pack[p * TAPS : (p + 1) * TAPS, :] = part[0:TAPS, p * LANES : (p + 1) * LANES]
    pack_sends = []
    for n, p in enumerate(dests):
        copy = remote(pack, pack_land.at[chip], bs_sem.at[n], br_sem.at[chip], p * 2 + core)
        copy.start()
        pack_sends.append(copy)
    pack_land[chip] = pack[...]
    returns += [give_back(1, n + FIRST, p, lag) for n, p in enumerate(dests[FIRST:])]

    for step in range(1, BLOCKS):
        source = lax.rem(me + BLOCKS - step, BLOCKS)
        arrived(squares_land.at[source], s1r_sem.at[source])
    total[...] = jnp.sum(squares_land[...], axis=0)
    total_sends = []
    for step in range(1, 8):
        copy = pltpu.make_async_remote_copy(
            src_ref=total, dst_ref=total_land.at[group], send_sem=s2s_sem.at[step],
            recv_sem=s2r_sem.at[group], device_id={"ch": lax.rem(group + step, 8)},
            device_id_type=MESH,
        )
        copy.start()
        total_sends.append(copy)
    total_land[group] = total[...]

    @pl.when(me < BLOCKS - 1)
    def _():
        arrived(tail, tail_sem.at[1])
        keyg[ROWS : ROWS + 8, :] = tail[...]

    @pl.when(me == BLOCKS - 1)
    def _():
        keyg[ROWS : ROWS + 8, :] = jnp.zeros((8, WIDTH), F32)

    def make_raw(p, carry):
        at = lanes(p)
        value = jnp.zeros((ROWS, LANES), F32)
        for j in range(TAPS):
            value = value + taps_ref[j : j + 1, at] * keyg[j : j + ROWS, at]
        krg[:, at] = value.astype(BF16)
        return carry

    lax.fori_loop(0, CHIPS, make_raw, 0)

    for source in sources:
        arrived(pack_land.at[source], br_sem.at[source])
    half_short[...] = jnp.sum(pack_land[...], axis=0)
    swap = remote(half_short, half_land, pack_sem.at[0], pack_sem.at[1], sibling)
    swap.start()
    for step in range(1, 8):
        source = lax.rem(group + 8 - step, 8)
        arrived(total_land.at[source], s2r_sem.at[source])
    total_all[...] = jnp.sum(total_land[...], axis=0)
    swap.wait()
    short[...] = half_short[...] + half_land[...]
    lag_keep.wait()
    for source in sources:
        arrived(lag.at[:, lanes(source)], rr_sem.at[1, source])

    for copies in (grad_sends, filter_sends, gated_sends, handed, returns):
        for copy in copies:
            copy.wait_send()
    for copies in (square_sends, pack_sends, total_sends):
        for copy in copies:
            copy.wait_send()

    @pl.when(me < BLOCKS - 1)
    def _():
        halo_copy().wait_send()

    @pl.when(me > 0)
    def _():
        tail_copy().wait_send()


def finish(qg, krg, vg, lag, total, short, qg_out, krg_out, vg_out, fg_out, sg_out, fg, sems):
    copies = [
        pltpu.make_async_copy(src, dst, sems.at[n])
        for n, (src, dst) in enumerate(((qg, qg_out), (krg, krg_out), (vg, vg_out)))
    ]
    for copy in copies:
        copy.start()
    everything = jnp.sum(total[...], axis=(0, 1), keepdims=True)
    scale = lax.rsqrt(everything / float(4096 * 8192) + 1e-06)
    rows = ROWS // FINISH_PARTS
    for n in range(FINISH_PARTS):
        at = pl.ds(n * rows, rows)
        fg[at, :] = lag[at, :].astype(F32) * scale
        copy = pltpu.make_async_copy(fg.at[at], fg_out.at[at], sems.at[3 + n])
        copy.start()
        copies.append(copy)
    for p in range(CHIPS):
        sg_out[:, p * LANES : (p + 1) * LANES] = short[p * TAPS : (p + 1) * TAPS, :]
    for copy in copies:
        copy.wait()


def per_device(query_branch, key_raw, value_branch, conv_out, out_grad, long_filter, short_filter):
    forward, inverse = tables()
    anywhere = pl.BlockSpec(memory_space=pl.ANY)
    in_hbm = pl.BlockSpec(memory_space=pltpu.HBM)
    in_vmem = pl.BlockSpec(memory_space=pltpu.VMEM)
    block = jax.ShapeDtypeStruct((ROWS, WIDTH), BF16)
    dma = pltpu.SemaphoreType.DMA
    vmem = pltpu.VMEM
    results = pl.pallas_call(
        kernel,
        out_shape=(
            *[vmem((ROWS, WIDTH), BF16)] * 4,
            vmem((8, LANES), F32),
            vmem((CHIPS * TAPS, LANES), F32),
        ),
        in_specs=[in_hbm] * 6 + [in_vmem] + [in_hbm] * 2,
        out_specs=(in_vmem,) * 6,
        scratch_shapes=[
            *[vmem((ROWS, WIDTH), BF16)] * 6,
            vmem((4 * ROWS, ROWS), BF16),
            vmem((2 * ROWS, 2 * ROWS), BF16),
            vmem((ROWS, WIDTH), BF16),
            vmem((ROWS, WIDTH), BF16),
            vmem((ROWS + 8, WIDTH), F32),
            vmem((ROWS, WIDTH), F32),
            vmem((16, WIDTH), BF16),
            vmem((3, CHIPS, ROWS, 2 * LANES), BF16),
            vmem((CHIPS + 1, 2 * ROWS, 2 * LANES), F32),
            vmem((CHIPS, ROWS, 2 * LANES), F32),
            vmem((CHIPS, 2 * ROWS, 2 * LANES), F32),
            vmem((CHIPS, ROWS, 2 * LANES), F32),
            vmem((2 * ROWS, CHIPS * LANES), BF16),
            vmem((2 * ROWS, CHIPS * LANES), BF16),
            vmem((2, CHIPS // 2, ROWS, 2 * LANES), BF16),
            vmem((ROWS, WIDTH), BF16),
            vmem((ROWS + 8, WIDTH), F32),
            vmem((8, WIDTH), F32),
            vmem((8, WIDTH), F32),
            vmem((CHIPS * TAPS, LANES), F32),
            vmem((CHIPS, CHIPS * TAPS, LANES), F32),
            vmem((CHIPS * TAPS, LANES), F32),
            vmem((CHIPS * TAPS, LANES), F32),
            vmem((8, LANES), F32),
            vmem((BLOCKS, 8, LANES), F32),
            vmem((8, LANES), F32),
            vmem((8, 8, LANES), F32),
            dma((8,)), dma((2,)), dma((2,)), dma((3, 8)), dma((3, 8)), dma((3, 8)), dma((3, 8)),
            dma((5,)), dma((2, 8)), dma((2, 8)),
            dma((2,)), dma((8,)), dma((8,)), dma((16,)), dma((16,)), dma((8,)), dma((8,)),
        ],
        compiler_params=pltpu.CompilerParams(
            collective_id=0, has_side_effects=True, vmem_limit_bytes=61 * 2**20
        ),
        cost_estimate=pl.CostEstimate(flops=6 * 10**9, bytes_accessed=7 * 2**20, transcendentals=0),
    )(
        query_branch, key_raw, value_branch, conv_out, out_grad, long_filter, short_filter,
        jnp.asarray(forward), jnp.asarray(inverse),
    )
    return pl.pallas_call(
        finish,
        out_shape=(
            block, block, block,
            jax.ShapeDtypeStruct((ROWS, WIDTH), F32),
            jax.ShapeDtypeStruct((TAPS, WIDTH), F32),
        ),
        in_specs=[in_vmem] * 6,
        out_specs=(anywhere, anywhere, anywhere, anywhere, in_vmem),
        scratch_shapes=[vmem((ROWS, WIDTH), F32), dma((3 + FINISH_PARTS,))],
        compiler_params=pltpu.CompilerParams(vmem_limit_bytes=8 * 2**20),
    )(*results)


def solution(mesh):
    both, taps = P("ctx", "ch"), P(None, "ch")
    return jax.shard_map(
        per_device,
        mesh=mesh,
        in_specs=(both,) * 6 + (taps,),
        out_specs=(both,) * 4 + (taps,),
        check_vma=False,
    )
```

```python
import functools

import jax
import jax.numpy as jnp
import ml_dtypes
import numpy as np
from jax import lax
from jax.experimental import pallas as pl
from jax.experimental.pallas import tpu as pltpu
from jax.sharding import PartitionSpec as P

MESH = pl.DeviceIdType.MESH
F32, BF16 = jnp.float32, jnp.bfloat16
ROWS, WIDTH, LANES, CHIPS, BLOCKS = 256, 1024, 128, 8, 16
TAPS = 3
FINISH_PARTS = 4
AHEAD = 3


def tables():
    length = 2 * ROWS
    rows = np.arange(length)
    freq = np.where(rows <= ROWS, rows, rows - ROWS)
    angle = (freq[:, None] * np.arange(ROWS)[None, :] % length) * (np.pi / ROWS)
    forward = np.where((rows <= ROWS)[:, None], np.cos(angle), -np.sin(angle))
    weight = np.where((freq == 0) | (freq == ROWS), 1.0, 2.0) / length
    inverse = forward.T * weight[None, :]

    def pair(table):
        upper = table.astype(ml_dtypes.bfloat16)
        lower = (table - upper.astype(np.float64)).astype(ml_dtypes.bfloat16)
        return np.concatenate([upper, lower], axis=0)

    return pair(forward), pair(inverse)


def lanes(index):
    return pl.ds(pl.multiple_of(index * LANES, LANES), LANES)


def kernel(
    qb_hbm, kr_hbm, vb_hbm, co_hbm, og_hbm, lf_hbm, taps_ref, fwd_hbm, inv_hbm,
    qg, krg, vg, lag, total_all, short,
    qb, kr, vb, co, og, lf, fwd, inv,
    cg, gated, ext, conv, halo, land, spec_g, sum_g, spec_a, dif_a,
    prod_hi, prod_lo, back, ret, keyg, tail,
    part, pack, pack_land, half_short, half_land, squares, squares_land, total, total_land,
    in_sem, halo_sem, tail_sem, send_sem, come_sem, pass_sem, other_sem, own_sem, rs_sem, rr_sem,
    pack_sem, bs_sem, br_sem, s1s_sem, s1r_sem, s2s_sem, s2r_sem,
):
    me = lax.axis_index("ctx")
    group = lax.axis_index("ch")
    chip, core = me // 2, lax.rem(me, 2)
    sibling = chip * 2 + 1 - core
    chip_x, chip_y = chip // 4, lax.rem(chip, 4)

    def chip_at(step, sign):
        dx, dy = lax.rem(step, 2), step // 2
        return lax.rem(chip_x + dx, 2) * 4 + lax.rem(chip_y + 4 + sign * dy, 4)

    dests = [chip_at(step, 1) for step in range(1, CHIPS)]
    sources = [chip_at(step, -1) for step in range(1, CHIPS)]
    mine, other = lanes(core), lanes(1 - core)

    def remote(src, dst, send, recv, ctx):
        return pltpu.make_async_remote_copy(
            src_ref=src, dst_ref=dst, send_sem=send, recv_sem=recv,
            device_id={"ctx": ctx}, device_id_type=MESH,
        )

    def arrived(ref, sem):
        pltpu.make_async_copy(ref, ref, sem).wait()

    loads = [
        pltpu.make_async_copy(src, dst, in_sem.at[n])
        for n, (src, dst) in enumerate(
            ((og_hbm, og), (qb_hbm, qb), (kr_hbm, kr), (lf_hbm, lf), (vb_hbm, vb),
             (fwd_hbm, fwd), (co_hbm, co), (inv_hbm, inv))
        )
    ]
    for load in loads:
        load.start()
    og_in, qb_in, kr_in, lf_in, vb_in, fwd_in, co_in, inv_in = loads

    barrier = pltpu.get_barrier_semaphore()
    for step in range(1, BLOCKS):
        pl.semaphore_signal(
            barrier, inc=1, device_id={"ctx": lax.rem(me + step, BLOCKS)}, device_id_type=MESH
        )
    for step in range(1, 8):
        pl.semaphore_signal(
            barrier, inc=1, device_id={"ch": lax.rem(group + step, 8)}, device_id_type=MESH
        )

    og_in.wait()
    qb_in.wait()

    def make_grad(p, carry):
        at = lanes(p)
        cg[:, at] = (og[:, at].astype(F32) * qb[:, at].astype(F32)).astype(BF16)
        return carry

    lax.fori_loop(0, CHIPS, make_grad, 0)
    kr_in.wait()
    lf_in.wait()
    pl.semaphore_wait(barrier, BLOCKS - 1 + 7)

    def halo_copy():
        return remote(
            kr.at[pl.ds(ROWS - 16, 16)], halo, halo_sem.at[0], halo_sem.at[1],
            lax.rem(me + 1, BLOCKS),
        )

    @pl.when(me < BLOCKS - 1)
    def _():
        halo_copy().start()

    def send_out(kind, block):
        copies = []
        for n, p in enumerate([chip] + dests):
            own = n == 0
            copies.append(
                remote(
                    block.at[:, lanes(p)], land.at[kind, chip, :, mine], send_sem.at[kind, n],
                    other_sem.at[kind, chip] if own else come_sem.at[kind, chip],
                    sibling if own else p * 2 + core,
                )
            )
            copies[-1].start()
        keep = pltpu.make_async_copy(
            block.at[:, lanes(chip)], land.at[kind, chip, :, mine], own_sem.at[kind]
        )
        keep.start()
        return copies, keep

    grad_sends, grad_keep = send_out(0, cg)
    filter_sends, filter_keep = send_out(1, lf)

    vb_in.wait()

    @pl.when(me > 0)
    def _():
        arrived(halo, halo_sem.at[1])
        ext[0:8, :] = halo[...].astype(F32)[8:16]

    @pl.when(me == 0)
    def _():
        ext[0:8, :] = jnp.zeros((8, WIDTH), F32)

    def make_gated(p, carry):
        at = lanes(p)
        ext[8:, at] = kr[:, at].astype(F32)
        value = jnp.zeros((ROWS, LANES), F32)
        for j in range(TAPS):
            value = value + taps_ref[j : j + 1, at] * ext[8 - j : 8 - j + ROWS, at]
        conv[:, at] = value
        gated[:, at] = (value * vb[:, at].astype(F32)).astype(BF16)
        return carry

    lax.fori_loop(0, CHIPS, make_gated, 0)
    gated_sends, gated_keep = send_out(2, gated)
    co_in.wait()

    def make_query(p, carry):
        at = lanes(p)
        qg[:, at] = (og[:, at].astype(F32) * co[:, at].astype(F32)).astype(BF16)
        return carry

    lax.fori_loop(0, CHIPS, make_query, 0)

    fwd_in.wait()

    def transform(block):
        twice = jnp.dot(fwd[...], block, preferred_element_type=F32)
        return twice[: 2 * ROWS] + twice[2 * ROWS :]

    def spectra(kind, keep, put, begin=False, begun=False):
        def pair(source):
            arrived(land.at[kind, source, :, other], other_sem.at[kind, source])
            put(source, transform(land[kind, source]))

        def handed(step):
            source = chip_at(step, -1)
            block = land.at[kind, source, :, mine]
            return remote(
                block, block, pass_sem.at[kind, step], other_sem.at[kind, source], sibling
            )

        def hand(step):
            source = chip_at(step, -1)
            arrived(land.at[kind, source, :, mine], come_sem.at[kind, source])
            handed(step).start()

        def turn(step, carry):
            @pl.when(step < CHIPS)
            def _():
                hand(step)

            pair(chip_at(step - AHEAD, -1))
            return carry

        if not begun:
            keep.wait()
            for step in range(1, AHEAD):
                hand(step)
        if begin:
            return None
        lax.fori_loop(AHEAD, CHIPS + AHEAD, turn, 0)
        return [handed(step) for step in range(1, CHIPS)]

    def put_grad(source, value):
        spec_g[source] = value

    def put_other(source, value):
        spec_a[source] = value
        dif_a[source] = value[:ROWS] - value[ROWS:]

    handed = spectra(0, grad_keep, put_grad)
    spec_g[CHIPS] = jnp.zeros((2 * ROWS, 2 * LANES), F32)

    def join_from(first):
        def join(m, carry):
            even = (lax.broadcasted_iota(jnp.int32, (2 * ROWS, LANES), 0) % 2) == 0
            for n in range(2):
                now, later = first + n, first + n + 1
                a = spec_g[m + now // 2, :, now % 2 * LANES : (now % 2 + 1) * LANES]
                b = spec_g[m + later // 2, :, later % 2 * LANES : (later % 2 + 1) * LANES]
                value = a + jnp.where(even, b, -b)
                at = slice(n * LANES, (n + 1) * LANES)
                spec_g[m, :, at] = value
                sum_g[m, :, at] = value[:ROWS] + value[ROWS:]
            return carry

        lax.fori_loop(0, CHIPS, join, 0)

    @pl.when(core == 0)
    def _():
        join_from(0)

    @pl.when(core == 1)
    def _():
        join_from(1)

    def products(half):
        base = 2 * half

        def turn(chunk, carry):
            halves = []
            for sub in range(2):
                row = pl.multiple_of(chunk * 16 + sub * 8, 8)
                re_at, im_at = pl.ds(row, 8), pl.ds(pl.multiple_of(row + ROWS, 8), 8)
                real, both, cross, held = [None] * 4, [None] * 4, [None] * 4, []
                for m in range(base, BLOCKS):
                    at = slice((m % 2) * LANES, (m % 2 + 1) * LANES)
                    g_re, g_im = spec_g[m // 2, re_at, at], spec_g[m // 2, im_at, at]
                    g_sum = sum_g[m // 2, re_at, at]
                    j = m - base
                    at = slice((j % 2) * LANES, (j % 2 + 1) * LANES)
                    held.append(
                        (spec_a[j // 2, re_at, at], spec_a[j // 2, im_at, at], dif_a[j // 2, re_at, at])
                    )
                    for u in range(min(4, j // 4 + 1)):
                        a_re, a_im, a_dif = held[j - 4 * u]
                        terms = (a_re * g_re, a_im * g_im, a_dif * g_sum)
                        for sums, term in zip((real, both, cross), terms):
                            sums[u] = term if sums[u] is None else sums[u] + term
                edge = (lax.broadcasted_iota(jnp.int32, (8, LANES), 0) + row) == 0
                halves.append(
                    [
                        (
                            jnp.where(edge, real[u], real[u] + both[u]),
                            jnp.where(edge, both[u], cross[u] - real[u] + both[u]),
                        )
                        for u in range(4)
                    ]
                )
            start = pl.multiple_of(chunk * 16, 16)
            for u in range(4):
                at = slice((half * 4 + u) * LANES, (half * 4 + u + 1) * LANES)
                for which, offset in ((0, 0), (1, ROWS)):
                    value = jnp.concatenate([halves[0][u][which], halves[1][u][which]], axis=0)
                    upper = value.astype(BF16)
                    rows_at = pl.ds(pl.multiple_of(start + offset, 16), 16)
                    prod_hi[rows_at, at] = upper
                    prod_lo[rows_at, at] = (value - upper.astype(F32)).astype(BF16)
            return carry

        lax.fori_loop(0, ROWS // 16, turn, 0)

    def restore(kind, half):
        at = slice(half * 4 * LANES, (half + 1) * 4 * LANES)
        twice = jnp.dot(inv[...], prod_hi[:, at], preferred_element_type=F32)
        result = twice[:ROWS] + twice[ROWS:]
        result = result + jnp.dot(inv[:ROWS], prod_lo[:, at], preferred_element_type=F32)
        for k in range(2):
            back[kind, half * 2 + k] = result[:, k * 2 * LANES : (k + 1) * 2 * LANES].astype(BF16)
        if kind == 1:
            square = result * result
            square = sum(square[:, k * LANES : (k + 1) * LANES] for k in range(4))
            squares[...] += jnp.sum(square.reshape(ROWS // 8, 8, LANES), axis=0)

    def back_copy(kind, half, step, goal):
        p = lax.rem(chip_x + step, 2) * 4 + lax.rem(chip_y // 2 + step // 2, 2) * 2 + half
        return remote(
            back.at[kind, half * 2 + p // 4, :, lanes(lax.rem(p, 4) // 2)], goal.at[:, lanes(chip)],
            rs_sem.at[kind, half * 4 + step], rr_sem.at[kind, chip], p * 2 + core,
        )

    def keep_back(kind, goal):
        return pltpu.make_async_copy(
            back.at[kind, lax.rem(chip, 2) * 2 + chip // 4, :, lanes(lax.rem(chip, 4) // 2)], goal.at[:, lanes(chip)],
            own_sem.at[3 + kind],
        )

    def give_back(kind, half, goal):
        for step in range(1, 4):
            back_copy(kind, half, step, goal).start()

        @pl.when(lax.rem(chip, 2) != half)
        def _():
            back_copy(kind, half, 0, goal).start()

        @pl.when(lax.rem(chip, 2) == half)
        def _():
            keep_back(kind, goal).start()

    def given_back(kind, half, goal):
        for step in range(1, 4):
            back_copy(kind, half, step, goal).wait_send()

        @pl.when(lax.rem(chip, 2) != half)
        def _():
            back_copy(kind, half, 0, goal).wait_send()

    handed = handed + spectra(1, filter_keep, put_other)
    inv_in.wait()
    for half in (1, 0):
        products(half)
        restore(0, half)
        give_back(0, half, ret)
        if half == 1:
            spectra(2, gated_keep, put_other, begin=True)

    handed = handed + spectra(2, gated_keep, put_other, begun=True)
    squares[...] = jnp.zeros((8, LANES), F32)
    products(1)
    restore(1, 1)
    give_back(1, 1, lag)
    products(0)
    restore(1, 0)

    square_sends = []
    for step in range(1, BLOCKS):
        copy = remote(
            squares, squares_land.at[me], s1s_sem.at[step], s1r_sem.at[me],
            lax.rem(me + step, BLOCKS),
        )
        copy.start()
        square_sends.append(copy)
    squares_land[me] = squares[...]

    part[...] = jnp.zeros((8, WIDTH), F32)

    def branch(source):
        at = lanes(source)
        wide = ret[:, at].astype(F32)
        vg[:, at] = (wide * conv[:, at]).astype(BF16)
        key = wide * vb[:, at].astype(F32)
        keyg[0:ROWS, at] = key
        for j in range(TAPS):
            part[j : j + 1, at] = jnp.sum(key * ext[8 - j : 8 - j + ROWS, at], axis=0, keepdims=True)

    def branch_turn(step, carry):
        source = chip_at(step, -1)
        arrived(ret.at[:, lanes(source)], rr_sem.at[0, source])
        branch(source)
        return carry

    keep_back(0, ret).wait()
    branch(chip)
    lax.fori_loop(1, CHIPS, branch_turn, 0)

    def tail_copy():
        return remote(
            keyg.at[pl.ds(0, 8)], tail, tail_sem.at[0], tail_sem.at[1],
            lax.rem(me + BLOCKS - 1, BLOCKS),
        )

    @pl.when(me > 0)
    def _():
        tail_copy().start()

    for p in range(CHIPS):
        pack[p * TAPS : (p + 1) * TAPS, :] = part[0:TAPS, p * LANES : (p + 1) * LANES]
    pack_sends = []
    for n, p in enumerate(dests):
        copy = remote(pack, pack_land.at[chip], bs_sem.at[n], br_sem.at[chip], p * 2 + core)
        copy.start()
        pack_sends.append(copy)
    pack_land[chip] = pack[...]
    give_back(1, 0, lag)

    def make_raw(start, rows):
        def turn(p, carry):
            at = lanes(p)
            value = jnp.zeros((rows, LANES), F32)
            for j in range(TAPS):
                value = value + taps_ref[j : j + 1, at] * keyg[start + j : start + j + rows, at]
            krg[start : start + rows, at] = value.astype(BF16)
            return carry

        return turn

    lax.fori_loop(0, CHIPS, make_raw(0, ROWS - 16), 0)

    for step in range(1, BLOCKS):
        source = lax.rem(me + BLOCKS - step, BLOCKS)
        arrived(squares_land.at[source], s1r_sem.at[source])
    total[...] = jnp.sum(squares_land[...], axis=0)
    total_sends = []
    for step in range(1, 8):
        copy = pltpu.make_async_remote_copy(
            src_ref=total, dst_ref=total_land.at[group], send_sem=s2s_sem.at[step],
            recv_sem=s2r_sem.at[group], device_id={"ch": lax.rem(group + step, 8)},
            device_id_type=MESH,
        )
        copy.start()
        total_sends.append(copy)
    total_land[group] = total[...]

    @pl.when(me < BLOCKS - 1)
    def _():
        arrived(tail, tail_sem.at[1])
        keyg[ROWS : ROWS + 8, :] = tail[...]

    @pl.when(me == BLOCKS - 1)
    def _():
        keyg[ROWS : ROWS + 8, :] = jnp.zeros((8, WIDTH), F32)

    lax.fori_loop(0, CHIPS, make_raw(ROWS - 16, 16), 0)

    for source in sources:
        arrived(pack_land.at[source], br_sem.at[source])
    half_short[...] = jnp.sum(pack_land[...], axis=0)
    swap = remote(half_short, half_land, pack_sem.at[0], pack_sem.at[1], sibling)
    swap.start()
    for step in range(1, 8):
        source = lax.rem(group + 8 - step, 8)
        arrived(total_land.at[source], s2r_sem.at[source])
    total_all[...] = jnp.sum(total_land[...], axis=0)
    swap.wait()
    short[...] = half_short[...] + half_land[...]
    keep_back(1, lag).wait()
    for source in sources:
        arrived(lag.at[:, lanes(source)], rr_sem.at[1, source])

    for copies in (grad_sends, filter_sends, gated_sends, handed):
        for copy in copies:
            copy.wait_send()
    for copies in (square_sends, pack_sends, total_sends):
        for copy in copies:
            copy.wait_send()

    for half in range(2):
        given_back(0, half, ret)
        given_back(1, half, lag)

    @pl.when(me < BLOCKS - 1)
    def _():
        halo_copy().wait_send()

    @pl.when(me > 0)
    def _():
        tail_copy().wait_send()


def finish(qg, krg, vg, lag, total, short, qg_out, krg_out, vg_out, fg_out, sg_out, fg, sems):
    copies = [
        pltpu.make_async_copy(src, dst, sems.at[n])
        for n, (src, dst) in enumerate(((qg, qg_out), (krg, krg_out), (vg, vg_out)))
    ]
    for copy in copies:
        copy.start()
    everything = jnp.sum(total[...], axis=(0, 1), keepdims=True)
    scale = lax.rsqrt(everything / float(4096 * 8192) + 1e-06)
    rows = ROWS // FINISH_PARTS
    for n in range(FINISH_PARTS):
        at = pl.ds(n * rows, rows)
        fg[at, :] = lag[at, :].astype(F32) * scale
        copy = pltpu.make_async_copy(fg.at[at], fg_out.at[at], sems.at[3 + n])
        copy.start()
        copies.append(copy)
    for p in range(CHIPS):
        sg_out[:, p * LANES : (p + 1) * LANES] = short[p * TAPS : (p + 1) * TAPS, :]
    for copy in copies:
        copy.wait()


def per_device(query_branch, key_raw, value_branch, conv_out, out_grad, long_filter, short_filter):
    forward, inverse = tables()
    anywhere = pl.BlockSpec(memory_space=pl.ANY)
    in_hbm = pl.BlockSpec(memory_space=pltpu.HBM)
    in_vmem = pl.BlockSpec(memory_space=pltpu.VMEM)
    block = jax.ShapeDtypeStruct((ROWS, WIDTH), BF16)
    dma = pltpu.SemaphoreType.DMA
    vmem = pltpu.VMEM
    results = pl.pallas_call(
        kernel,
        out_shape=(
            *[vmem((ROWS, WIDTH), BF16)] * 4,
            vmem((8, LANES), F32),
            vmem((CHIPS * TAPS, LANES), F32),
        ),
        in_specs=[in_hbm] * 6 + [in_vmem] + [in_hbm] * 2,
        out_specs=(in_vmem,) * 6,
        scratch_shapes=[
            *[vmem((ROWS, WIDTH), BF16)] * 6,
            vmem((4 * ROWS, ROWS), BF16),
            vmem((2 * ROWS, 2 * ROWS), BF16),
            vmem((ROWS, WIDTH), BF16),
            vmem((ROWS, WIDTH), BF16),
            vmem((ROWS + 8, WIDTH), F32),
            vmem((ROWS, WIDTH), F32),
            vmem((16, WIDTH), BF16),
            vmem((3, CHIPS, ROWS, 2 * LANES), BF16),
            vmem((CHIPS + 1, 2 * ROWS, 2 * LANES), F32),
            vmem((CHIPS, ROWS, 2 * LANES), F32),
            vmem((CHIPS, 2 * ROWS, 2 * LANES), F32),
            vmem((CHIPS, ROWS, 2 * LANES), F32),
            vmem((2 * ROWS, CHIPS * LANES), BF16),
            vmem((2 * ROWS, CHIPS * LANES), BF16),
            vmem((2, CHIPS // 2, ROWS, 2 * LANES), BF16),
            vmem((ROWS, WIDTH), BF16),
            vmem((ROWS + 8, WIDTH), F32),
            vmem((8, WIDTH), F32),
            vmem((8, WIDTH), F32),
            vmem((CHIPS * TAPS, LANES), F32),
            vmem((CHIPS, CHIPS * TAPS, LANES), F32),
            vmem((CHIPS * TAPS, LANES), F32),
            vmem((CHIPS * TAPS, LANES), F32),
            vmem((8, LANES), F32),
            vmem((BLOCKS, 8, LANES), F32),
            vmem((8, LANES), F32),
            vmem((8, 8, LANES), F32),
            dma((8,)), dma((2,)), dma((2,)), dma((3, 8)), dma((3, 8)), dma((3, 8)), dma((3, 8)),
            dma((5,)), dma((2, 8)), dma((2, 8)),
            dma((2,)), dma((8,)), dma((8,)), dma((16,)), dma((16,)), dma((8,)), dma((8,)),
        ],
        compiler_params=pltpu.CompilerParams(
            collective_id=0, has_side_effects=True, vmem_limit_bytes=61 * 2**20
        ),
        cost_estimate=pl.CostEstimate(flops=6 * 10**9, bytes_accessed=7 * 2**20, transcendentals=0),
    )(
        query_branch, key_raw, value_branch, conv_out, out_grad, long_filter, short_filter,
        jnp.asarray(forward), jnp.asarray(inverse),
    )
    return pl.pallas_call(
        finish,
        out_shape=(
            block, block, block,
            jax.ShapeDtypeStruct((ROWS, WIDTH), F32),
            jax.ShapeDtypeStruct((TAPS, WIDTH), F32),
        ),
        in_specs=[in_vmem] * 6,
        out_specs=(anywhere, anywhere, anywhere, anywhere, in_vmem),
        scratch_shapes=[vmem((ROWS, WIDTH), F32), dma((3 + FINISH_PARTS,))],
        compiler_params=pltpu.CompilerParams(vmem_limit_bytes=8 * 2**20),
    )(*results)


def solution(mesh):
    both, taps = P("ctx", "ch"), P(None, "ch")
    return jax.shard_map(
        per_device,
        mesh=mesh,
        in_specs=(both,) * 6 + (taps,),
        out_specs=(both,) * 4 + (taps,),
        check_vma=False,
    )
```

```python
import functools

import jax
import jax.numpy as jnp
import ml_dtypes
import numpy as np
from jax import lax
from jax.experimental import pallas as pl
from jax.experimental.pallas import tpu as pltpu
from jax.sharding import PartitionSpec as P

MESH = pl.DeviceIdType.MESH
F32, BF16 = jnp.float32, jnp.bfloat16
ROWS, WIDTH, LANES, CHIPS, BLOCKS = 256, 1024, 128, 8, 16
TAPS = 3
FINISH_PARTS = 4
AHEAD = 3


def tables():
    length = 2 * ROWS
    rows = np.arange(length)
    freq = np.where(rows <= ROWS, rows, rows - ROWS)
    angle = (freq[:, None] * np.arange(ROWS)[None, :] % length) * (np.pi / ROWS)
    forward = np.where((rows <= ROWS)[:, None], np.cos(angle), -np.sin(angle))
    weight = np.where((freq == 0) | (freq == ROWS), 1.0, 2.0) / length
    inverse = forward.T * weight[None, :]

    def pair(table):
        upper = table.astype(ml_dtypes.bfloat16)
        lower = (table - upper.astype(np.float64)).astype(ml_dtypes.bfloat16)
        return np.concatenate([upper, lower], axis=0)

    return pair(forward), pair(inverse)


def lanes(index):
    return pl.ds(pl.multiple_of(index * LANES, LANES), LANES)


def kernel(
    qb_hbm, kr_hbm, vb_hbm, co_hbm, og_hbm, lf_hbm, taps_ref, fwd_hbm, inv_hbm,
    qg, krg, vg, lag, total_all, short,
    qb, kr, vb, co, og, lf, fwd, inv,
    cg, gated, ext, conv, halo, land, spec_g, sum_g, spec_a, dif_a,
    prod_hi, prod_lo, back, ret, keyg, tail,
    part, pack, pack_land, half_short, half_land, squares, squares_land, total, total_land,
    in_sem, halo_sem, tail_sem, send_sem, come_sem, pass_sem, other_sem, own_sem, rs_sem, rr_sem,
    pack_sem, bs_sem, br_sem, s1s_sem, s1r_sem, s2s_sem, s2r_sem,
):
    me = lax.axis_index("ctx")
    group = lax.axis_index("ch")
    chip, core = me // 2, lax.rem(me, 2)
    sibling = chip * 2 + 1 - core
    chip_x, chip_y = chip // 4, lax.rem(chip, 4)

    def chip_at(step, sign):
        dx, dy = lax.rem(step, 2), step // 2
        return lax.rem(chip_x + dx, 2) * 4 + lax.rem(chip_y + 4 + sign * dy, 4)

    dests = [chip_at(step, 1) for step in range(1, CHIPS)]
    sources = [chip_at(step, -1) for step in range(1, CHIPS)]
    mine, other = lanes(core), lanes(1 - core)

    def remote(src, dst, send, recv, ctx):
        return pltpu.make_async_remote_copy(
            src_ref=src, dst_ref=dst, send_sem=send, recv_sem=recv,
            device_id={"ctx": ctx}, device_id_type=MESH,
        )

    def arrived(ref, sem):
        pltpu.make_async_copy(ref, ref, sem).wait()

    loads = [
        pltpu.make_async_copy(src, dst, in_sem.at[n])
        for n, (src, dst) in enumerate(
            ((og_hbm, og), (qb_hbm, qb), (kr_hbm, kr), (lf_hbm, lf), (vb_hbm, vb),
             (fwd_hbm, fwd), (co_hbm, co), (inv_hbm, inv))
        )
    ]
    for load in loads:
        load.start()
    og_in, qb_in, kr_in, lf_in, vb_in, fwd_in, co_in, inv_in = loads

    barrier = pltpu.get_barrier_semaphore()
    for step in range(1, BLOCKS):
        pl.semaphore_signal(
            barrier, inc=1, device_id={"ctx": lax.rem(me + step, BLOCKS)}, device_id_type=MESH
        )
    for step in range(1, 8):
        pl.semaphore_signal(
            barrier, inc=1, device_id={"ch": lax.rem(group + step, 8)}, device_id_type=MESH
        )

    og_in.wait()
    qb_in.wait()

    def make_grad(p, carry):
        at = lanes(p)
        cg[:, at] = (og[:, at].astype(F32) * qb[:, at].astype(F32)).astype(BF16)
        return carry

    lax.fori_loop(0, CHIPS, make_grad, 0)
    kr_in.wait()
    lf_in.wait()
    pl.semaphore_wait(barrier, BLOCKS - 1 + 7)

    def halo_copy():
        return remote(
            kr.at[pl.ds(ROWS - 16, 16)], halo, halo_sem.at[0], halo_sem.at[1],
            lax.rem(me + 1, BLOCKS),
        )

    @pl.when(me < BLOCKS - 1)
    def _():
        halo_copy().start()

    def send_out(kind, block):
        copies = []
        for n, p in enumerate([chip] + dests):
            own = n == 0
            copies.append(
                remote(
                    block.at[:, lanes(p)], land.at[kind, chip, :, mine], send_sem.at[kind, n],
                    other_sem.at[kind, chip] if own else come_sem.at[kind, chip],
                    sibling if own else p * 2 + core,
                )
            )
            copies[-1].start()
        keep = pltpu.make_async_copy(
            block.at[:, lanes(chip)], land.at[kind, chip, :, mine], own_sem.at[kind]
        )
        keep.start()
        return copies, keep

    grad_sends, grad_keep = send_out(0, cg)
    filter_sends, filter_keep = send_out(1, lf)

    vb_in.wait()

    @pl.when(me > 0)
    def _():
        arrived(halo, halo_sem.at[1])
        ext[0:8, :] = halo[...].astype(F32)[8:16]

    @pl.when(me == 0)
    def _():
        ext[0:8, :] = jnp.zeros((8, WIDTH), F32)

    def make_gated(p, carry):
        at = lanes(p)
        ext[8:, at] = kr[:, at].astype(F32)
        value = jnp.zeros((ROWS, LANES), F32)
        for j in range(TAPS):
            value = value + taps_ref[j : j + 1, at] * ext[8 - j : 8 - j + ROWS, at]
        conv[:, at] = value
        gated[:, at] = (value * vb[:, at].astype(F32)).astype(BF16)
        return carry

    lax.fori_loop(0, CHIPS, make_gated, 0)
    gated_sends, gated_keep = send_out(2, gated)
    co_in.wait()

    def make_query(p, carry):
        at = lanes(p)
        qg[:, at] = (og[:, at].astype(F32) * co[:, at].astype(F32)).astype(BF16)
        return carry

    lax.fori_loop(0, CHIPS, make_query, 0)

    fwd_in.wait()

    def transform(block):
        twice = jnp.dot(fwd[...], block, preferred_element_type=F32)
        return twice[: 2 * ROWS] + twice[2 * ROWS :]

    def spectra(kind, keep, put, begin=False, begun=False):
        def pair(source):
            arrived(land.at[kind, source, :, other], other_sem.at[kind, source])
            put(source, transform(land[kind, source]))

        def handed(step):
            source = chip_at(step, -1)
            block = land.at[kind, source, :, mine]
            return remote(
                block, block, pass_sem.at[kind, step], other_sem.at[kind, source], sibling
            )

        def hand(step):
            source = chip_at(step, -1)
            arrived(land.at[kind, source, :, mine], come_sem.at[kind, source])
            handed(step).start()

        def turn(step, carry):
            @pl.when(step < CHIPS)
            def _():
                hand(step)

            pair(chip_at(step - AHEAD, -1))
            return carry

        if not begun:
            keep.wait()
            for step in range(1, AHEAD):
                hand(step)
        if begin:
            return None
        lax.fori_loop(AHEAD, CHIPS + AHEAD, turn, 0)
        return [handed(step) for step in range(1, CHIPS)]

    def put_grad(source, value):
        spec_g[source] = value

    def put_other(source, value):
        spec_a[source] = value
        dif_a[source] = value[:ROWS] - value[ROWS:]

    handed = spectra(0, grad_keep, put_grad)
    spec_g[CHIPS] = jnp.zeros((2 * ROWS, 2 * LANES), F32)

    spectra(1, filter_keep, put_other, begin=True)

    def join_from(first):
        def join(m, carry):
            even = (lax.broadcasted_iota(jnp.int32, (2 * ROWS, LANES), 0) % 2) == 0
            for n in range(2):
                now, later = first + n, first + n + 1
                a = spec_g[m + now // 2, :, now % 2 * LANES : (now % 2 + 1) * LANES]
                b = spec_g[m + later // 2, :, later % 2 * LANES : (later % 2 + 1) * LANES]
                value = a + jnp.where(even, b, -b)
                at = slice(n * LANES, (n + 1) * LANES)
                spec_g[m, :, at] = value
                sum_g[m, :, at] = value[:ROWS] + value[ROWS:]
            return carry

        lax.fori_loop(0, CHIPS, join, 0)

    @pl.when(core == 0)
    def _():
        join_from(0)

    @pl.when(core == 1)
    def _():
        join_from(1)

    def products(half):
        base = 2 * half

        def turn(chunk, carry):
            halves = []
            for sub in range(2):
                row = pl.multiple_of(chunk * 16 + sub * 8, 8)
                re_at, im_at = pl.ds(row, 8), pl.ds(pl.multiple_of(row + ROWS, 8), 8)
                real, both, cross, held = [None] * 4, [None] * 4, [None] * 4, []
                for m in range(base, BLOCKS):
                    at = slice((m % 2) * LANES, (m % 2 + 1) * LANES)
                    g_re, g_im = spec_g[m // 2, re_at, at], spec_g[m // 2, im_at, at]
                    g_sum = sum_g[m // 2, re_at, at]
                    j = m - base
                    at = slice((j % 2) * LANES, (j % 2 + 1) * LANES)
                    held.append(
                        (spec_a[j // 2, re_at, at], spec_a[j // 2, im_at, at], dif_a[j // 2, re_at, at])
                    )
                    for u in range(min(4, j // 4 + 1)):
                        a_re, a_im, a_dif = held[j - 4 * u]
                        terms = (a_re * g_re, a_im * g_im, a_dif * g_sum)
                        for sums, term in zip((real, both, cross), terms):
                            sums[u] = term if sums[u] is None else sums[u] + term
                edge = (lax.broadcasted_iota(jnp.int32, (8, LANES), 0) + row) == 0
                halves.append(
                    [
                        (
                            jnp.where(edge, real[u], real[u] + both[u]),
                            jnp.where(edge, both[u], cross[u] - real[u] + both[u]),
                        )
                        for u in range(4)
                    ]
                )
            start = pl.multiple_of(chunk * 16, 16)
            for u in range(4):
                at = slice((half * 4 + u) * LANES, (half * 4 + u + 1) * LANES)
                for which, offset in ((0, 0), (1, ROWS)):
                    value = jnp.concatenate([halves[0][u][which], halves[1][u][which]], axis=0)
                    upper = value.astype(BF16)
                    rows_at = pl.ds(pl.multiple_of(start + offset, 16), 16)
                    prod_hi[rows_at, at] = upper
                    prod_lo[rows_at, at] = (value - upper.astype(F32)).astype(BF16)
            return carry

        lax.fori_loop(0, ROWS // 16, turn, 0)

    def restore(kind, half):
        at = slice(half * 4 * LANES, (half + 1) * 4 * LANES)
        twice = jnp.dot(inv[...], prod_hi[:, at], preferred_element_type=F32)
        result = twice[:ROWS] + twice[ROWS:]
        result = result + jnp.dot(inv[:ROWS], prod_lo[:, at], preferred_element_type=F32)
        for k in range(2):
            back[kind, half * 2 + k] = result[:, k * 2 * LANES : (k + 1) * 2 * LANES].astype(BF16)
        if kind == 1:
            square = result * result
            square = sum(square[:, k * LANES : (k + 1) * LANES] for k in range(4))
            squares[...] += jnp.sum(square.reshape(ROWS // 8, 8, LANES), axis=0)

    def back_copy(kind, half, step, goal):
        p = lax.rem(chip_x + step, 2) * 4 + lax.rem(chip_y // 2 + step // 2, 2) * 2 + half
        return remote(
            back.at[kind, half * 2 + p // 4, :, lanes(lax.rem(p, 4) // 2)], goal.at[:, lanes(chip)],
            rs_sem.at[kind, half * 4 + step], rr_sem.at[kind, chip], p * 2 + core,
        )

    def keep_back(kind, goal):
        return pltpu.make_async_copy(
            back.at[kind, lax.rem(chip, 2) * 2 + chip // 4, :, lanes(lax.rem(chip, 4) // 2)], goal.at[:, lanes(chip)],
            own_sem.at[3 + kind],
        )

    def give_back(kind, half, goal):
        for step in range(1, 4):
            back_copy(kind, half, step, goal).start()

        @pl.when(lax.rem(chip, 2) != half)
        def _():
            back_copy(kind, half, 0, goal).start()

        @pl.when(lax.rem(chip, 2) == half)
        def _():
            keep_back(kind, goal).start()

    def given_back(kind, half, goal):
        for step in range(1, 4):
            back_copy(kind, half, step, goal).wait_send()

        @pl.when(lax.rem(chip, 2) != half)
        def _():
            back_copy(kind, half, 0, goal).wait_send()

    handed = handed + spectra(1, filter_keep, put_other, begun=True)
    inv_in.wait()
    for half in (1, 0):
        products(half)
        restore(0, half)
        give_back(0, half, ret)
        if half == 1:
            spectra(2, gated_keep, put_other, begin=True)

    handed = handed + spectra(2, gated_keep, put_other, begun=True)
    squares[...] = jnp.zeros((8, LANES), F32)
    products(1)
    restore(1, 1)
    give_back(1, 1, lag)
    products(0)
    restore(1, 0)

    square_sends = []
    for step in range(1, BLOCKS):
        copy = remote(
            squares, squares_land.at[me], s1s_sem.at[step], s1r_sem.at[me],
            lax.rem(me + step, BLOCKS),
        )
        copy.start()
        square_sends.append(copy)
    squares_land[me] = squares[...]

    part[...] = jnp.zeros((8, WIDTH), F32)

    def branch(source):
        at = lanes(source)
        wide = ret[:, at].astype(F32)
        vg[:, at] = (wide * conv[:, at]).astype(BF16)
        key = wide * vb[:, at].astype(F32)
        keyg[0:ROWS, at] = key
        for j in range(TAPS):
            part[j : j + 1, at] = jnp.sum(key * ext[8 - j : 8 - j + ROWS, at], axis=0, keepdims=True)

    def branch_turn(step, carry):
        source = chip_at(step, -1)
        arrived(ret.at[:, lanes(source)], rr_sem.at[0, source])
        branch(source)
        return carry

    keep_back(0, ret).wait()
    branch(chip)
    lax.fori_loop(1, CHIPS, branch_turn, 0)

    def tail_copy():
        return remote(
            keyg.at[pl.ds(0, 8)], tail, tail_sem.at[0], tail_sem.at[1],
            lax.rem(me + BLOCKS - 1, BLOCKS),
        )

    @pl.when(me > 0)
    def _():
        tail_copy().start()

    for p in range(CHIPS):
        pack[p * TAPS : (p + 1) * TAPS, :] = part[0:TAPS, p * LANES : (p + 1) * LANES]
    pack_sends = []
    for n, p in enumerate(dests):
        copy = remote(pack, pack_land.at[chip], bs_sem.at[n], br_sem.at[chip], p * 2 + core)
        copy.start()
        pack_sends.append(copy)
    pack_land[chip] = pack[...]
    give_back(1, 0, lag)

    def make_raw(start, rows):
        def turn(p, carry):
            at = lanes(p)
            value = jnp.zeros((rows, LANES), F32)
            for j in range(TAPS):
                value = value + taps_ref[j : j + 1, at] * keyg[start + j : start + j + rows, at]
            krg[start : start + rows, at] = value.astype(BF16)
            return carry

        return turn

    lax.fori_loop(0, CHIPS, make_raw(0, ROWS - 16), 0)

    for step in range(1, BLOCKS):
        source = lax.rem(me + BLOCKS - step, BLOCKS)
        arrived(squares_land.at[source], s1r_sem.at[source])
    total[...] = jnp.sum(squares_land[...], axis=0)
    total_sends = []
    for step in range(1, 8):
        copy = pltpu.make_async_remote_copy(
            src_ref=total, dst_ref=total_land.at[group], send_sem=s2s_sem.at[step],
            recv_sem=s2r_sem.at[group], device_id={"ch": lax.rem(group + step, 8)},
            device_id_type=MESH,
        )
        copy.start()
        total_sends.append(copy)
    total_land[group] = total[...]

    @pl.when(me < BLOCKS - 1)
    def _():
        arrived(tail, tail_sem.at[1])
        keyg[ROWS : ROWS + 8, :] = tail[...]

    @pl.when(me == BLOCKS - 1)
    def _():
        keyg[ROWS : ROWS + 8, :] = jnp.zeros((8, WIDTH), F32)

    lax.fori_loop(0, CHIPS, make_raw(ROWS - 16, 16), 0)

    for source in sources:
        arrived(pack_land.at[source], br_sem.at[source])
    half_short[...] = jnp.sum(pack_land[...], axis=0)
    swap = remote(half_short, half_land, pack_sem.at[0], pack_sem.at[1], sibling)
    swap.start()
    for step in range(1, 8):
        source = lax.rem(group + 8 - step, 8)
        arrived(total_land.at[source], s2r_sem.at[source])
    total_all[...] = jnp.sum(total_land[...], axis=0)
    swap.wait()
    short[...] = half_short[...] + half_land[...]
    keep_back(1, lag).wait()
    for source in sources:
        arrived(lag.at[:, lanes(source)], rr_sem.at[1, source])

    for copies in (grad_sends, filter_sends, gated_sends, handed):
        for copy in copies:
            copy.wait_send()
    for copies in (square_sends, pack_sends, total_sends):
        for copy in copies:
            copy.wait_send()

    for half in range(2):
        given_back(0, half, ret)
        given_back(1, half, lag)

    @pl.when(me < BLOCKS - 1)
    def _():
        halo_copy().wait_send()

    @pl.when(me > 0)
    def _():
        tail_copy().wait_send()


def finish(qg, krg, vg, lag, total, short, qg_out, krg_out, vg_out, fg_out, sg_out, fg, sems):
    copies = [
        pltpu.make_async_copy(src, dst, sems.at[n])
        for n, (src, dst) in enumerate(((qg, qg_out), (krg, krg_out), (vg, vg_out)))
    ]
    for copy in copies:
        copy.start()
    everything = jnp.sum(total[...], axis=(0, 1), keepdims=True)
    scale = lax.rsqrt(everything / float(4096 * 8192) + 1e-06)
    rows = ROWS // FINISH_PARTS
    for n in range(FINISH_PARTS):
        at = pl.ds(n * rows, rows)
        fg[at, :] = lag[at, :].astype(F32) * scale
        copy = pltpu.make_async_copy(fg.at[at], fg_out.at[at], sems.at[3 + n])
        copy.start()
        copies.append(copy)
    for p in range(CHIPS):
        sg_out[:, p * LANES : (p + 1) * LANES] = short[p * TAPS : (p + 1) * TAPS, :]
    for copy in copies:
        copy.wait()


def per_device(query_branch, key_raw, value_branch, conv_out, out_grad, long_filter, short_filter):
    forward, inverse = tables()
    anywhere = pl.BlockSpec(memory_space=pl.ANY)
    in_hbm = pl.BlockSpec(memory_space=pltpu.HBM)
    in_vmem = pl.BlockSpec(memory_space=pltpu.VMEM)
    block = jax.ShapeDtypeStruct((ROWS, WIDTH), BF16)
    dma = pltpu.SemaphoreType.DMA
    vmem = pltpu.VMEM
    results = pl.pallas_call(
        kernel,
        out_shape=(
            *[vmem((ROWS, WIDTH), BF16)] * 4,
            vmem((8, LANES), F32),
            vmem((CHIPS * TAPS, LANES), F32),
        ),
        in_specs=[in_hbm] * 6 + [in_vmem] + [in_hbm] * 2,
        out_specs=(in_vmem,) * 6,
        scratch_shapes=[
            *[vmem((ROWS, WIDTH), BF16)] * 6,
            vmem((4 * ROWS, ROWS), BF16),
            vmem((2 * ROWS, 2 * ROWS), BF16),
            vmem((ROWS, WIDTH), BF16),
            vmem((ROWS, WIDTH), BF16),
            vmem((ROWS + 8, WIDTH), F32),
            vmem((ROWS, WIDTH), F32),
            vmem((16, WIDTH), BF16),
            vmem((3, CHIPS, ROWS, 2 * LANES), BF16),
            vmem((CHIPS + 1, 2 * ROWS, 2 * LANES), F32),
            vmem((CHIPS, ROWS, 2 * LANES), F32),
            vmem((CHIPS, 2 * ROWS, 2 * LANES), F32),
            vmem((CHIPS, ROWS, 2 * LANES), F32),
            vmem((2 * ROWS, CHIPS * LANES), BF16),
            vmem((2 * ROWS, CHIPS * LANES), BF16),
            vmem((2, CHIPS // 2, ROWS, 2 * LANES), BF16),
            vmem((ROWS, WIDTH), BF16),
            vmem((ROWS + 8, WIDTH), F32),
            vmem((8, WIDTH), F32),
            vmem((8, WIDTH), F32),
            vmem((CHIPS * TAPS, LANES), F32),
            vmem((CHIPS, CHIPS * TAPS, LANES), F32),
            vmem((CHIPS * TAPS, LANES), F32),
            vmem((CHIPS * TAPS, LANES), F32),
            vmem((8, LANES), F32),
            vmem((BLOCKS, 8, LANES), F32),
            vmem((8, LANES), F32),
            vmem((8, 8, LANES), F32),
            dma((8,)), dma((2,)), dma((2,)), dma((3, 8)), dma((3, 8)), dma((3, 8)), dma((3, 8)),
            dma((5,)), dma((2, 8)), dma((2, 8)),
            dma((2,)), dma((8,)), dma((8,)), dma((16,)), dma((16,)), dma((8,)), dma((8,)),
        ],
        compiler_params=pltpu.CompilerParams(
            collective_id=0, has_side_effects=True, vmem_limit_bytes=61 * 2**20
        ),
        cost_estimate=pl.CostEstimate(flops=6 * 10**9, bytes_accessed=7 * 2**20, transcendentals=0),
    )(
        query_branch, key_raw, value_branch, conv_out, out_grad, long_filter, short_filter,
        jnp.asarray(forward), jnp.asarray(inverse),
    )
    return pl.pallas_call(
        finish,
        out_shape=(
            block, block, block,
            jax.ShapeDtypeStruct((ROWS, WIDTH), F32),
            jax.ShapeDtypeStruct((TAPS, WIDTH), F32),
        ),
        in_specs=[in_vmem] * 6,
        out_specs=(anywhere, anywhere, anywhere, anywhere, in_vmem),
        scratch_shapes=[vmem((ROWS, WIDTH), F32), dma((3 + FINISH_PARTS,))],
        compiler_params=pltpu.CompilerParams(vmem_limit_bytes=8 * 2**20),
    )(*results)


def solution(mesh):
    both, taps = P("ctx", "ch"), P(None, "ch")
    return jax.shard_map(
        per_device,
        mesh=mesh,
        in_specs=(both,) * 6 + (taps,),
        out_specs=(both,) * 4 + (taps,),
        check_vma=False,
    )
```
